512 devices in a mesh: grp: 8 (over x, z_lo), blk: 64 (over y, z_hi, core).
Axes of the slice: x: 4, y: 8, z: 8 (z_hi: 4, z_lo: 2; z = z_hi * 2 + z_lo), core: 2. Of those that a mesh axis runs over, the one named last changes fastest.
Arguments:
- queries: bfloat16 [512, 64, 128], P(('grp', 'blk')), may hold values from -120 to 120
- prefix_kv: bfloat16 [2, 8, 65536, 128], P(None, 'grp', 'blk'), may hold values from -6 to 6
- suffix_kv: bfloat16 [512, 256, 2, 4, 128], P(('grp', 'blk')), may hold values from -8 to 8
- new_kv: bfloat16 [512, 2, 4, 128], P(('grp', 'blk')), may hold values from -5 to 5
- suffix_len: int32 [512], P(('grp', 'blk')), may hold values from 1 to 256, as said below
Outputs:
- attended: bfloat16 [512, 64, 128], P(('grp', 'blk'))
The draws below stay inside these ranges and needn't reach their ends.
Inputs may be any that keep to these rules, and one draw needn't show every extreme that they name: `suffix_len`: some request has all 256 positions live in every draw.
All inputs are finite; a program needn't handle non-finite values.
Results may differ from the reference program's by a relative error of at most 0.0044.
Values may be sent and summed in bfloat16 or wider, within the bound.
A program may use at most 64 MiB of HBM per device.

```python
import jax
import jax.numpy as jnp
from jax import lax

H = 64
KVH = 4
HD = 128
SL = 256
S_MAX = 256
REQ = 512
GSPAN = 16384
PREFIX = 131072
N_GRP = 8


def common_draw(key):
    fresh_key = jax.random.fold_in(key, 101)
    new_pair = jnp.clip(jax.random.normal(fresh_key, (REQ, 2, KVH, HD), jnp.float32), -5.0, 5.0)
    return new_pair


def draw_new_kv(key, part):
    new_pair = common_draw(key)
    return new_pair.astype(jnp.bfloat16)


def draw_queries(key, part):
    new_pair = common_draw(key)
    key = jax.random.fold_in(key, 3)
    expand = jnp.repeat(new_pair[:, 0], H // KVH, axis=1)
    result = 3.0 * jnp.clip(jax.random.normal(key, (REQ, H, HD), jnp.float32), -5.0, 5.0) + expand
    return result.astype(jnp.bfloat16)


def draw_suffix_kv(key, part):
    new_pair = common_draw(key)
    key = jax.random.fold_in(key, 5)
    base = jnp.clip(jax.random.normal(key, (REQ, S_MAX, 2, KVH, HD), jnp.float32), -5.0, 5.0)
    cache_keys = base[:, :, 0] + 0.5 * new_pair[:, None, 0]
    return jnp.stack([cache_keys, base[:, :, 1]], axis=2).astype(jnp.bfloat16)


def draw_suffix_len(key, part):
    key = jax.random.fold_in(key, 7)
    lengths = jax.random.randint(key, (REQ,), 1, S_MAX + 1)
    longest = jax.random.randint(jax.random.fold_in(key, 1), (), 0, REQ)
    return jnp.where(jnp.arange(REQ) == longest, S_MAX, lengths).astype(jnp.int32)


def steps_of(key, dims, cuts, least, top_value):
    factor_of, own = 1.0, jax.random.fold_in(key, 6)
    for axis_at, parts in cuts:
        draws = jnp.exp(jax.random.uniform(jax.random.fold_in(own, axis_at), (parts,), jnp.float32, least / len(cuts), top_value / len(cuts)))
        factor_of = factor_of * jnp.repeat(draws, dims[axis_at] // parts).reshape([-1 if axis == axis_at else 1 for axis in range(len(dims))])
    return factor_of


def gaussian(key, extent, width, most, split=(), kind=jnp.bfloat16):
    entries = width * jax.random.normal(key, extent, jnp.float32)
    if split:
        entries = entries * steps_of(key, extent, split, -0.22, 0.18)
    return jnp.clip(entries, -most, most).astype(kind)


def setup_inputs(seed: int = 0) -> dict:
    seeds = jax.random.split(jax.random.key(seed), 6)
    return {
        "queries": draw_queries(jax.random.fold_in(seeds[5], 71), 0),
        "prefix_kv": gaussian(seeds[1], (2, N_GRP, KVH * GSPAN, HD), 1.0, 6.0, ((1, 8), (2, 64))),
        "suffix_kv": draw_suffix_kv(jax.random.fold_in(seeds[5], 71), 0),
        "new_kv": draw_new_kv(jax.random.fold_in(seeds[5], 71), 0),
        "suffix_len": draw_suffix_len(jax.random.fold_in(seeds[5], 71), 0),
    }


def combine(first, second):
    best_score = jnp.maximum(first[2], second[2])
    early = jnp.exp(first[2] - best_score)
    later = jnp.exp(second[2] - best_score)
    numerator = first[0] * early[..., None] + second[0] * later[..., None]
    denominator = first[1] * early + second[1] * later
    return (numerator, denominator, best_score)


def block_partial(grouped, key_block_tiles, block_values):
    scores = jnp.einsum('rgpd,gkd->rgpk', grouped, key_block_tiles.astype(jnp.float32)) * (HD ** -0.5)
    best_score = jnp.max(scores, -1)
    softmax_weight = lax.optimization_barrier(jnp.exp(scores - best_score[..., None]).astype(jnp.bfloat16)).astype(jnp.float32)
    denominator = jnp.sum(softmax_weight, -1)
    numerator = jnp.einsum('rgpk,gkd->rgpd', softmax_weight, block_values.astype(jnp.float32))
    return (numerator, denominator, best_score)


def suffix_partial(grouped, suffix_kv, new_kv, suffix_len):
    reciprocal_scale = HD ** -0.5
    cache_keys = suffix_kv[:, :, 0].astype(jnp.float32)
    stored_value_rows = suffix_kv[:, :, 1].astype(jnp.float32)
    scores = jnp.einsum('rgpd,rsgd->rgps', grouped, cache_keys) * reciprocal_scale
    inside = jnp.arange(S_MAX, dtype=jnp.int32)[None, :] < suffix_len[:, None]
    scores = jnp.where(inside[:, None, None, :], scores, -jnp.inf)
    own_score = jnp.einsum('rgpd,rgd->rgp', grouped, new_kv[:, 0].astype(jnp.float32)) * reciprocal_scale
    best_score = jnp.maximum(jnp.max(scores, -1), own_score)
    softmax_weight = lax.optimization_barrier(jnp.exp(scores - best_score[..., None]).astype(jnp.bfloat16)).astype(jnp.float32)
    own_weight = lax.optimization_barrier(jnp.exp(own_score - best_score).astype(jnp.bfloat16)).astype(jnp.float32)
    denominator = jnp.sum(softmax_weight, -1) + own_weight
    numerator = jnp.einsum('rgps,rsgd->rgpd', softmax_weight, stored_value_rows)
    numerator = numerator + own_weight[..., None] * new_kv[:, 1].astype(jnp.float32)[:, :, None, :]
    return (numerator, denominator, best_score)


def reference(queries, prefix_kv, suffix_kv, new_kv, suffix_len):
    grouped = queries.astype(jnp.float32).reshape(REQ, KVH, H // KVH, HD)
    ordered = prefix_kv.reshape(2, N_GRP, KVH, GSPAN, HD)
    ordered = jnp.transpose(ordered, (0, 2, 1, 3, 4)).reshape(2, KVH, PREFIX, HD)
    running = suffix_partial(grouped, suffix_kv, new_kv, suffix_len)

    def absorb(running, block_index):
        offset = block_index * SL
        key_block_tiles = lax.dynamic_slice_in_dim(ordered[0], offset, SL, 1)
        block_values = lax.dynamic_slice_in_dim(ordered[1], offset, SL, 1)
        return combine(running, block_partial(grouped, key_block_tiles, block_values)), None

    running, unused = lax.scan(absorb, running, jnp.arange(PREFIX // SL, dtype=jnp.int32))
    numerator, denominator, best_score = running
    return (numerator / denominator[..., None]).reshape(REQ, H, HD).astype(jnp.bfloat16)
```

```python
import functools

import jax
import jax.numpy as jnp
from jax import lax
from jax.experimental import pallas as pl
from jax.experimental.pallas import tpu as pltpu
from jax.sharding import PartitionSpec as P

MESH = pl.DeviceIdType.MESH
H, KVH, HD = 64, 4, 128
SHARE = H // KVH
NX, NY, NZ = 4, 8, 8
KEYS = 1024
HALF = KEYS // 2
CHUNK = 256
BLOCK = NY * SHARE
ROWS = NZ * BLOCK
S_MAX = 256
SUF = S_MAX * 2 * KVH
SCALE = HD**-0.5 * 1.4426950408889634
STAT = 16
RING = (0, 1, 7, 2, 6, 3, 5, 4)
NEAR = 5
F32, BF16 = jnp.float32, jnp.bfloat16


def place(x, y, z, core):
    return (x * 2 + z % 2, y * 8 + (z // 2) * 2 + core)


def dot_t(a, b):
    return lax.dot_general(a, b, (((1,), (1,)), ((), ())), preferred_element_type=F32)


def to_lanes(column, rows):
    row = lax.broadcasted_iota(jnp.int32, (rows, 128), 0)
    lane = lax.broadcasted_iota(jnp.int32, (rows, 128), 1)
    return jnp.sum(jnp.where(row == lane, column, 0.0), 0, keepdims=True)


def to_rows(line, rows):
    row = lax.broadcasted_iota(jnp.int32, (rows, 128), 0)
    lane = lax.broadcasted_iota(jnp.int32, (rows, 128), 1)
    return jnp.sum(jnp.where(row == lane, line, 0.0), 1, keepdims=True)


def split3(value):
    high = value.astype(BF16).astype(F32)
    middle = (value - high).astype(BF16).astype(F32)
    return high, middle, value - high - middle


def merge(parts):
    best = functools.reduce(jnp.maximum, [p[1] for p in parts])
    weights = [jnp.exp2(p[1] - best) for p in parts]
    total = functools.reduce(jnp.add, weights)
    mixed = functools.reduce(jnp.add, [w * p[0] for w, p in zip(weights, parts)])
    return mixed / total, best + jnp.log2(total)


def suffix_part(q, cached, fresh, length):
    head = lax.broadcasted_iota(jnp.int32, (H, 128), 0) // SHARE
    lane = lax.broadcasted_iota(jnp.int32, (H, 128), 1)
    mine = lane % (2 * KVH) == head
    pieces = SUF // 128
    per_piece = 128 // (2 * KVH)
    low = -jnp.inf
    scores = dot_t(q, cached) * SCALE
    slices = [
        jnp.where(
            mine & (lane // (2 * KVH) + i * per_piece < length),
            scores[:, i * 128 : (i + 1) * 128],
            low,
        )
        for i in range(pieces)
    ]
    slices.append(
        jnp.where(mine & (lane < 2 * KVH), dot_t(q, fresh) * SCALE, low)
    )
    best = jnp.max(functools.reduce(jnp.maximum, slices), -1, keepdims=True)
    weights = [jnp.exp2(s - best).astype(BF16).astype(F32) for s in slices]
    total = jnp.sum(functools.reduce(jnp.add, weights), -1, keepdims=True)
    moved = [pltpu.roll(w, KVH, 1).astype(BF16) for w in weights]
    out = jnp.dot(
        jnp.concatenate(moved[:pieces], 1), cached, preferred_element_type=F32
    ) + jnp.dot(moved[pieces], fresh, preferred_element_type=F32)
    return out / total, best + jnp.log2(total)


def kernel(
    q_ref, kv_ref, suffix_ref, fresh_ref, length_ref, out_ref,
    qall, kvb, cached, fresh, num, den, top, outgoing, returned, ysend, yback,
    y_sem, z_sem, k_sem, zo_sem, yo_sem, local_sem,
):
    g, b = lax.axis_index("grp"), lax.axis_index("blk")
    x, z = g // 2, (b % 8) // 2 * 2 + g % 2
    y, core = b // 8, b % 2

    def along_x(d):
        return place((x + d) % NX, y, z, core)

    def along_y(d):
        return place(x, (y + d) % NY, z, core)

    def along_z(d):
        return place(x, y, (z + d) % NZ, core)

    other = place(x, y, z, 1 - core)

    def remote(src, dst, sems, i, device):
        return pltpu.make_async_remote_copy(
            src_ref=src, dst_ref=dst, send_sem=sems.at[0, i], recv_sem=sems.at[1, i],
            device_id=device, device_id_type=MESH,
        )

    barrier = pltpu.get_barrier_semaphore()
    partners = [along_x(1), along_x(3), other]
    for d in range(1, 8):
        partners += [along_y(d), along_z(d)]
    for device in partners:
        pl.semaphore_signal(barrier, inc=1, device_id=device, device_id_type=MESH)
    own_kv = pltpu.make_async_copy(kv_ref, kvb.at[0, 0], local_sem.at[0])
    own_kv.start()
    own_suffix = pltpu.make_async_copy(suffix_ref, cached, local_sem.at[1])
    own_suffix.start()
    pl.semaphore_wait(barrier, len(partners))

    y_copies = []
    for k in (7, 5, 6, 3, 4, 1, 2):
        d = RING[k]
        rows = pl.ds(pl.multiple_of((y + d) % NY // 2 * SHARE, SHARE), SHARE)
        y_copies.append(
            (k, remote(q_ref.at[rows], qall.at[0, pl.ds(k * SHARE, SHARE)], y_sem, k, along_y(d)))
        )
        y_copies[-1][1].start()
    mine = pl.ds(pl.multiple_of(y // 2 * SHARE, SHARE), SHARE)
    qall[0, 0:SHARE, :] = q_ref[mine, :]

    first, second = pl.ds(0, HALF), pl.ds(HALF, HALF)
    halves = (first, second)
    own_kv.wait()
    kv_copies = {}

    def kv_send(name, src, dst, device):
        i = len(kv_copies)
        kv_copies[name] = remote(src, dst, k_sem, i, device)
        kv_copies[name].start()

    def piece(slot, side, half):
        return kvb.at[slot, side, :, halves[half]]

    kv_send("right0", piece(0, 0, 0), piece(3, 0, 0), along_x(1))
    kv_send("left1", piece(0, 0, 1), piece(1, 0, 1), along_x(3))
    kv_send("pair", kvb.at[0, 0], kvb.at[0, 1], other)
    kv_send("right1", piece(0, 0, 1), piece(3, 0, 1), along_x(1))
    kv_send("left0", piece(0, 0, 0), piece(1, 0, 0), along_x(3))

    z_copies = []
    for batch, (lo, hi) in enumerate(((0, NEAR), (NEAR, NY))):
        for k, copy in y_copies:
            if lo <= k < hi:
                copy.wait_recv()
        rows = pl.ds(lo * SHARE, (hi - lo) * SHARE)
        for k in (7, 5, 6, 3, 4, 1, 2):
            copy = remote(
                qall.at[0, rows], qall.at[k, rows], z_sem, batch * 8 + k, along_z(RING[k])
            )
            copy.start()
            z_copies.append(copy)

    own_suffix.wait()
    fresh[...] = jnp.zeros_like(fresh)
    fresh[0 : 2 * KVH, :] = fresh_ref[...]
    suffix_out, suffix_log = suffix_part(q_ref[...], cached[...], fresh[...], length_ref[0])

    def forward(name, slot, half):
        kv_send(name, piece(slot, 0, half), piece(slot, 1, half), other)

    kv_copies["right0"].wait_recv()
    kv_send("relay0", piece(3, 0, 0), piece(2, 0, 0), along_x(1))
    forward("pair30", 3, 0)
    kv_copies["left1"].wait_recv()
    kv_send("relay1", piece(1, 0, 1), piece(2, 0, 1), along_x(3))
    forward("pair11", 1, 1)

    def absorb(units, state):
        q = qall[...].reshape(ROWS, HD)
        for slot, side, half in units:
            for j in range(HALF // CHUNK):
                at = half * HALF + j * CHUNK
                keys = kvb[slot, side, 0, at : at + CHUNK, :]
                values = kvb[slot, side, 1, at : at + CHUNK, :]
                s = dot_t(q, keys) * SCALE
                best = jnp.max(s, -1, keepdims=True)
                if state is not None:
                    best = jnp.maximum(best, state[2])
                w = jnp.exp2(s - best).astype(BF16)
                n = jnp.dot(w, values, preferred_element_type=F32)
                t = w[:, :128].astype(F32) + w[:, 128:].astype(F32)
                if state is not None:
                    keep = jnp.exp2(state[2] - best)
                    n = n + state[0] * keep
                    t = t + state[1] * keep
                state = (n, t, best)
        return state

    def load():
        return num[...], den[...], top[...][:, :1]

    def save(state):
        num[...], den[...] = state[0], state[1]
        top[...] = jnp.broadcast_to(state[2], (ROWS, 128))

    for copy in z_copies:
        copy.wait_recv()
    save(absorb([(0, 0, 0), (0, 0, 1)], None))
    kv_copies["pair"].wait_recv()
    save(absorb([(0, 1, 0), (0, 1, 1)], load()))
    save(absorb([(3, 0, 0), (1, 0, 1)], load()))
    kv_copies["right1"].wait_recv()
    forward("pair31", 3, 1)
    kv_copies["left0"].wait_recv()
    forward("pair10", 1, 0)
    kv_copies["pair30"].wait_recv()
    kv_copies["pair11"].wait_recv()
    save(absorb([(3, 1, 0), (1, 1, 1)], load()))
    save(absorb([(3, 0, 1), (1, 0, 0)], load()))
    kv_copies["relay0"].wait_recv()
    forward("pair20", 2, 0)
    kv_copies["relay1"].wait_recv()
    forward("pair21", 2, 1)
    kv_copies["pair31"].wait_recv()
    kv_copies["pair10"].wait_recv()
    save(absorb([(3, 1, 1), (1, 1, 0)], load()))
    save(absorb([(2, 0, 0), (2, 0, 1)], load()))
    kv_copies["pair20"].wait_recv()
    kv_copies["pair21"].wait_recv()
    save(absorb([(2, 1, 0), (2, 1, 1)], load()))

    def normal(k):
        rows = slice(k * BLOCK, (k + 1) * BLOCK)
        total = jnp.sum(den[rows, :], -1, keepdims=True)
        return num[rows, :] / total, top[rows, :] + jnp.log2(total)

    zo_copies = []
    for k in (7, 5, 6, 3, 4, 1, 2):
        average, log = normal(k)
        outgoing[k, 0:BLOCK, :] = average.astype(BF16)
        lines = jnp.concatenate(
            [*split3(to_lanes(log, BLOCK)), jnp.zeros((STAT - 3, 128), F32)], 0
        )
        outgoing[k, BLOCK : BLOCK + STAT, :] = lines.astype(BF16)
        copy = remote(outgoing.at[k], returned.at[k], zo_sem, k, along_z(8 - RING[k]))
        copy.start()
        zo_copies.append((k, copy))
    parts = [normal(0)]
    for k, copy in reversed(zo_copies):
        copy.wait_recv()
        lines = returned[k, BLOCK : BLOCK + STAT, :].astype(F32)
        line = lines[0:1] + lines[1:2] + lines[2:3]
        parts.append((returned[k, 0:BLOCK, :].astype(F32), to_rows(line, BLOCK)))
    average, log = merge(parts)
    log = jnp.broadcast_to(log, (BLOCK, 128))

    yo_copies = []
    for k in (7, 5, 6, 3, 4, 1, 2, 0):
        rows = slice(k * SHARE, (k + 1) * SHARE)
        line = to_lanes(log[rows], SHARE)
        message = jnp.concatenate([average[rows], jnp.broadcast_to(line, (8, 128))], 0)
        if k == 0:
            yback[y] = message
        else:
            ysend[k] = message
            copy = remote(ysend.at[k], yback.at[y], yo_sem, k, along_y(8 - RING[k]))
            copy.start()
            yo_copies.append(copy)
    for copy in yo_copies:
        copy.wait_recv()
    for head in range(KVH):
        rows = slice(head * SHARE, (head + 1) * SHARE)
        parts = [(suffix_out[rows], suffix_log[rows])]
        for member in (2 * head, 2 * head + 1):
            message = yback[member]
            parts.append((message[:SHARE], to_rows(message[SHARE : SHARE + 1], SHARE)))
        out_ref[rows, :] = merge(parts)[0].astype(BF16)

    for copy in [c for _, c in y_copies] + z_copies + list(kv_copies.values()):
        copy.wait_send()
    for copy in [c for _, c in zo_copies] + yo_copies:
        copy.wait_send()


def local(queries, prefix_kv, suffix_kv, new_kv, suffix_len):
    dma = pltpu.SemaphoreType.DMA
    vmem = pl.BlockSpec(memory_space=pltpu.VMEM)
    hbm = pl.BlockSpec(memory_space=pl.ANY)
    out = pl.pallas_call(
        kernel,
        out_shape=jax.ShapeDtypeStruct((H, HD), BF16),
        in_specs=[vmem, hbm, hbm, vmem, pl.BlockSpec(memory_space=pltpu.SMEM)],
        out_specs=vmem,
        scratch_shapes=[
            pltpu.VMEM((NZ, BLOCK, HD), BF16),
            pltpu.VMEM((NX, 2, 2, KEYS, HD), BF16),
            pltpu.VMEM((SUF, HD), BF16),
            pltpu.VMEM((128, HD), BF16),
            pltpu.VMEM((ROWS, HD), F32),
            pltpu.VMEM((ROWS, 128), F32),
            pltpu.VMEM((ROWS, 128), F32),
            pltpu.VMEM((NZ, BLOCK + STAT, HD), BF16),
            pltpu.VMEM((NZ, BLOCK + STAT, HD), BF16),
            pltpu.VMEM((NY, SHARE + 8, HD), F32),
            pltpu.VMEM((NY, SHARE + 8, HD), F32),
            dma((2, 8)),
            dma((2, 16)),
            dma((2, 13)),
            dma((2, 8)),
            dma((2, 8)),
            dma((2,)),
        ],
        compiler_params=pltpu.CompilerParams(
            collective_id=0, has_side_effects=True, vmem_limit_bytes=56 * 2**20
        ),
    )(
        queries.reshape(H, HD),
        prefix_kv.reshape(2, KEYS, HD),
        suffix_kv.reshape(SUF, HD),
        new_kv.reshape(2 * KVH, HD),
        suffix_len,
    )
    return out.reshape(1, H, HD)


def solution(mesh):
    in_specs = (
        P(("grp", "blk"), None, None),
        P(None, "grp", "blk", None),
        P(("grp", "blk"), None, None, None, None),
        P(("grp", "blk"), None, None, None),
        P(("grp", "blk")),
    )
    out_specs = P(("grp", "blk"), None, None)
    return jax.shard_map(local, mesh=mesh, in_specs=in_specs, out_specs=out_specs, check_vma=False)
```

```python
import functools

import jax
import jax.numpy as jnp
from jax import lax
from jax.experimental import pallas as pl
from jax.experimental.pallas import tpu as pltpu
from jax.sharding import PartitionSpec as P

MESH = pl.DeviceIdType.MESH
H, KVH, HD = 64, 4, 128
SHARE = H // KVH
NX, NY, NZ = 4, 8, 8
KEYS = 1024
HALF = KEYS // 2
CHUNK = 256
BLOCK = NY * SHARE
ROWS = NZ * BLOCK
S_MAX = 256
SUF = S_MAX * 2 * KVH
SCALE = HD**-0.5 * 1.4426950408889634
STAT = 16
PART = ROWS // 2
LOWEST = -1e30
RING = (0, 1, 7, 2, 6, 3, 5, 4)
NEAR = 5
K_NAMES = (
    "right0", "left1", "pair", "relay0", "relay1", "right1", "left0",
    "f10", "f11", "f20", "f21", "f30", "f31",
)
F32, BF16 = jnp.float32, jnp.bfloat16


def place(x, y, z, core):
    return (x * 2 + z % 2, y * 8 + (z // 2) * 2 + core)


def dot_t(a, b):
    return lax.dot_general(a, b, (((1,), (1,)), ((), ())), preferred_element_type=F32)


def to_lanes(column, rows):
    row = lax.broadcasted_iota(jnp.int32, (rows, 128), 0)
    lane = lax.broadcasted_iota(jnp.int32, (rows, 128), 1)
    return jnp.sum(jnp.where(row == lane, column, 0.0), 0, keepdims=True)


def to_rows(line, rows):
    row = lax.broadcasted_iota(jnp.int32, (rows, 128), 0)
    lane = lax.broadcasted_iota(jnp.int32, (rows, 128), 1)
    return jnp.sum(jnp.where(row == lane, line, 0.0), 1, keepdims=True)


def split3(value):
    high = value.astype(BF16).astype(F32)
    middle = (value - high).astype(BF16).astype(F32)
    return high, middle, value - high - middle


def merge(parts):
    best = functools.reduce(jnp.maximum, [p[1] for p in parts])
    weights = [jnp.exp2(p[1] - best) for p in parts]
    total = functools.reduce(jnp.add, weights)
    mixed = functools.reduce(jnp.add, [w * p[0] for w, p in zip(weights, parts)])
    return mixed / total, best + jnp.log2(total)


def suffix_part(q, cached, fresh, length):
    head = lax.broadcasted_iota(jnp.int32, (H, 128), 0) // SHARE
    lane = lax.broadcasted_iota(jnp.int32, (H, 128), 1)
    mine = lane % (2 * KVH) == head
    pieces = SUF // 128
    per_piece = 128 // (2 * KVH)
    low = -jnp.inf
    scores = dot_t(q, cached) * SCALE
    slices = [
        jnp.where(
            mine & (lane // (2 * KVH) + i * per_piece < length),
            scores[:, i * 128 : (i + 1) * 128],
            low,
        )
        for i in range(pieces)
    ]
    slices.append(
        jnp.where(mine & (lane < 2 * KVH), dot_t(q, fresh) * SCALE, low)
    )
    best = jnp.max(functools.reduce(jnp.maximum, slices), -1, keepdims=True)
    weights = [jnp.exp2(s - best).astype(BF16).astype(F32) for s in slices]
    total = jnp.sum(functools.reduce(jnp.add, weights), -1, keepdims=True)
    moved = [pltpu.roll(w, KVH, 1).astype(BF16) for w in weights]
    out = jnp.dot(
        jnp.concatenate(moved[:pieces], 1), cached, preferred_element_type=F32
    ) + jnp.dot(moved[pieces], fresh, preferred_element_type=F32)
    return out / total, best + jnp.log2(total)


def kernel(
    q_ref, kv_ref, suffix_ref, fresh_ref, length_ref, out_ref,
    qall, kvb, cached, fresh, num, den, top, outgoing, returned, ysend, yback,
    y_sem, z_sem, k_sem, zo_sem, yo_sem, local_sem,
):
    def shifted(dx, dy, dz, dcore):
        g, b = lax.axis_index("grp"), lax.axis_index("blk")
        x, z = g // 2, (b % 8) // 2 * 2 + g % 2
        y, core = b // 8, b % 2
        return place((x + dx) % NX, (y + dy) % NY, (z + dz) % NZ, (core + dcore) % 2)

    def along_x(d):
        return shifted(d, 0, 0, 0)

    def along_y(d):
        return shifted(0, d, 0, 0)

    def along_z(d):
        return shifted(0, 0, d, 0)

    y = lax.axis_index("blk") // 8

    def remote(src, dst, sems, i, device):
        return pltpu.make_async_remote_copy(
            src_ref=src, dst_ref=dst, send_sem=sems.at[0, i], recv_sem=sems.at[1, i],
            device_id=device, device_id_type=MESH,
        )

    def kv_copy(name):
        own = {
            "right0": ((0, 0, 0), (1, 0, 0), along_x(1)),
            "left1": ((0, 0, 1), (1, 0, 1), along_x(3)),
            "pair": ((0, 0), (0, 1), shifted(0, 0, 0, 1)),
            "relay0": ((1, 0, 0), (2, 0, 0), along_x(1)),
            "relay1": ((1, 0, 1), (2, 0, 1), along_x(3)),
            "right1": ((0, 0, 1), (3, 0, 0), along_x(1)),
            "left0": ((0, 0, 0), (3, 0, 1), along_x(3)),
        }
        for stage in (1, 2, 3):
            for which in (0, 1):
                own[f"f{stage}{which}"] = (
                    (stage, 0, which), (stage, 1, which), shifted(0, 0, 0, 1)
                )
        src, dst, device = own[name]
        return remote(kvb.at[src], kvb.at[dst], k_sem, K_NAMES.index(name), device)

    def kv_send(*names):
        for name in names:
            kv_copy(name).start()

    def kv_wait(*names):
        for name in names:
            kv_copy(name).wait_recv()

    def z_copy(k, batch):
        lo, hi = ((0, NEAR), (NEAR, NY))[batch]
        rows = pl.ds(lo * SHARE, (hi - lo) * SHARE)
        return remote(
            qall.at[0, rows], qall.at[k, rows], z_sem, batch * 8 + k, along_z(RING[k])
        )

    def zo_copy(k):
        return remote(outgoing.at[k], returned.at[k], zo_sem, k, along_z(8 - RING[k]))

    barrier = pltpu.get_barrier_semaphore()
    partners = [along_x(1), along_x(3), shifted(0, 0, 0, 1)]
    for d in range(1, 8):
        partners += [along_y(d), along_z(d)]
    for device in partners:
        pl.semaphore_signal(barrier, inc=1, device_id=device, device_id_type=MESH)
    own_kv = [
        pltpu.make_async_copy(kv_ref.at[:, pl.ds(h * HALF, HALF)], kvb.at[0, 0, h], local_sem.at[h])
        for h in range(2)
    ]
    for copy in own_kv:
        copy.start()
    own_suffix = pltpu.make_async_copy(suffix_ref, cached, local_sem.at[2])
    own_suffix.start()
    pl.semaphore_wait(barrier, len(partners))

    y_copies = []
    for k in (7, 5, 6, 3, 4, 1, 2):
        d = RING[k]
        rows = pl.ds(pl.multiple_of((y + d) % NY // 2 * SHARE, SHARE), SHARE)
        y_copies.append(
            (k, remote(q_ref.at[rows], qall.at[0, pl.ds(k * SHARE, SHARE)], y_sem, k, along_y(d)))
        )
        y_copies[-1][1].start()
    mine = pl.ds(pl.multiple_of(y // 2 * SHARE, SHARE), SHARE)
    qall[0, 0:SHARE, :] = q_ref[mine, :]

    for copy in own_kv:
        copy.wait()
    kv_send("right0", "left1", "pair")

    for batch, (lo, hi) in enumerate(((0, NEAR), (NEAR, NY))):
        for k, copy in y_copies:
            if lo <= k < hi:
                copy.wait_recv()
        for k in (7, 5, 6, 3, 4, 1, 2):
            z_copy(k, batch).start()

    kv_wait("right0")
    kv_send("relay0")
    kv_wait("left1")
    kv_send("relay1", "right1", "left0", "f10", "f11")

    own_suffix.wait()
    fresh[...] = jnp.zeros_like(fresh)
    fresh[0 : 2 * KVH, :] = fresh_ref[...]
    suffix_out, suffix_log = suffix_part(q_ref[...], cached[...], fresh[...], length_ref[0])

    def absorb(part, stage):
        rows = pl.ds(pl.multiple_of(part * PART, PART), PART)
        q = qall[pl.ds(part * (NZ // 2), NZ // 2)].reshape(PART, HD)
        n, t, best = num[rows, :], den[rows, :], top[rows, :]
        for side in range(2):
            for which in range(2):
                for j in range(HALF // CHUNK):
                    at = slice(j * CHUNK, (j + 1) * CHUNK)
                    keys = kvb[stage, side, which, 0, at, :]
                    values = kvb[stage, side, which, 1, at, :]
                    s = dot_t(q, keys) * SCALE
                    s = [s[:, i : i + 128] for i in range(0, CHUNK, 128)]
                    peak = jnp.max(functools.reduce(jnp.maximum, s), -1, keepdims=True)
                    peak = jnp.maximum(jnp.broadcast_to(peak, (PART, 128)), best)
                    w = [jnp.exp2(i - peak).astype(BF16) for i in s]
                    keep = jnp.exp2(best - peak)
                    n = n * keep + jnp.dot(
                        jnp.concatenate(w, 1), values, preferred_element_type=F32
                    )
                    t = t * keep + functools.reduce(jnp.add, [i.astype(F32) for i in w])
                    best = peak
        num[rows, :], den[rows, :], top[rows, :] = n, t, best

    def normal(k):
        rows = slice(k * BLOCK, (k + 1) * BLOCK)
        total = jnp.broadcast_to(jnp.sum(den[rows, :], -1, keepdims=True), (BLOCK, 128))
        return num[rows, :] / total, top[rows, :] + jnp.log2(total)

    def give_back(blocks):
        for k in blocks:
            average, log = normal(k)
            outgoing[k, 0:BLOCK, :] = average.astype(BF16)
            lines = jnp.concatenate(
                [*split3(to_lanes(log, BLOCK)), jnp.zeros((STAT - 3, 128), F32)], 0
            )
            outgoing[k, BLOCK : BLOCK + STAT, :] = lines.astype(BF16)
            zo_copy(k).start()

    num[...] = jnp.zeros_like(num)
    den[...] = jnp.zeros_like(den)
    top[...] = jnp.full(top.shape, LOWEST, F32)
    for k in range(1, NZ // 2):
        z_copy(k, 0).wait_recv()
        z_copy(k, 1).wait_recv()
    kv_wait("pair")

    @pl.loop(0, 4)
    def _(i):
        @pl.when(i == 1)
        def _():
            kv_wait("f10", "f11")

        @pl.when(i == 2)
        def _():
            for k in range(NZ // 2, NZ):
                z_copy(k, 0).wait_recv()
                z_copy(k, 1).wait_recv()

        @pl.when(i == 3)
        def _():
            kv_wait("relay0", "relay1")
            kv_send("f20", "f21")

        absorb(i // 2, i % 2)

    @pl.loop(0, 4)
    def _(i):
        @pl.when(i == 0)
        def _():
            kv_wait("f20", "f21")

        @pl.when(i == 1)
        def _():
            kv_wait("right1", "left0")
            kv_send("f30", "f31")

        @pl.when(i == 2)
        def _():
            kv_wait("f30", "f31")

        @pl.when(i == 3)
        def _():
            give_back((7, 5, 6, 4))

        absorb(1 - i % 2, 2 + i // 2)

    give_back((3, 1, 2))
    parts = [normal(0)]
    for k in (7, 5, 6, 4, 1, 2, 3):
        zo_copy(k).wait_recv()
        lines = returned[k, BLOCK : BLOCK + STAT, :].astype(F32)
        line = lines[0:1] + lines[1:2] + lines[2:3]
        log = jnp.broadcast_to(to_rows(line, BLOCK), (BLOCK, 128))
        parts.append((returned[k, 0:BLOCK, :].astype(F32), log))
    average, log = merge(parts)

    yo_copies = []
    for k in (7, 5, 6, 3, 4, 1, 2, 0):
        rows = slice(k * SHARE, (k + 1) * SHARE)
        line = to_lanes(log[rows], SHARE)
        message = jnp.concatenate([average[rows], jnp.broadcast_to(line, (8, 128))], 0)
        if k == 0:
            yback[y] = message
        else:
            ysend[k] = message
            copy = remote(ysend.at[k], yback.at[y], yo_sem, k, along_y(8 - RING[k]))
            copy.start()
            yo_copies.append(copy)
    for copy in yo_copies:
        copy.wait_recv()
    for head in range(KVH):
        rows = slice(head * SHARE, (head + 1) * SHARE)
        parts = [(suffix_out[rows], suffix_log[rows])]
        for member in (2 * head, 2 * head + 1):
            message = yback[member]
            parts.append((message[:SHARE], to_rows(message[SHARE : SHARE + 1], SHARE)))
        out_ref[rows, :] = merge(parts)[0].astype(BF16)

    for copy in [c for _, c in y_copies] + yo_copies:
        copy.wait_send()
    for k in range(1, NZ):
        z_copy(k, 0).wait_send()
        z_copy(k, 1).wait_send()
        zo_copy(k).wait_send()
    for name in K_NAMES:
        kv_copy(name).wait_send()


def local(queries, prefix_kv, suffix_kv, new_kv, suffix_len):
    dma = pltpu.SemaphoreType.DMA
    vmem = pl.BlockSpec(memory_space=pltpu.VMEM)
    hbm = pl.BlockSpec(memory_space=pl.ANY)
    out = pl.pallas_call(
        kernel,
        out_shape=jax.ShapeDtypeStruct((H, HD), BF16),
        in_specs=[vmem, hbm, hbm, vmem, pl.BlockSpec(memory_space=pltpu.SMEM)],
        out_specs=vmem,
        scratch_shapes=[
            pltpu.VMEM((NZ, BLOCK, HD), BF16),
            pltpu.VMEM((NX, 2, 2, 2, HALF, HD), BF16),
            pltpu.VMEM((SUF, HD), BF16),
            pltpu.VMEM((128, HD), BF16),
            pltpu.VMEM((ROWS, HD), F32),
            pltpu.VMEM((ROWS, 128), F32),
            pltpu.VMEM((ROWS, 128), F32),
            pltpu.VMEM((NZ, BLOCK + STAT, HD), BF16),
            pltpu.VMEM((NZ, BLOCK + STAT, HD), BF16),
            pltpu.VMEM((NY, SHARE + 8, HD), F32),
            pltpu.VMEM((NY, SHARE + 8, HD), F32),
            dma((2, 8)),
            dma((2, 16)),
            dma((2, 13)),
            dma((2, 8)),
            dma((2, 8)),
            dma((3,)),
        ],
        compiler_params=pltpu.CompilerParams(
            collective_id=0, has_side_effects=True, vmem_limit_bytes=56 * 2**20
        ),
    )(
        queries.reshape(H, HD),
        prefix_kv.reshape(2, KEYS, HD),
        suffix_kv.reshape(SUF, HD),
        new_kv.reshape(2 * KVH, HD),
        suffix_len,
    )
    return out.reshape(1, H, HD)


def solution(mesh):
    in_specs = (
        P(("grp", "blk"), None, None),
        P(None, "grp", "blk", None),
        P(("grp", "blk"), None, None, None, None),
        P(("grp", "blk"), None, None, None),
        P(("grp", "blk")),
    )
    out_specs = P(("grp", "blk"), None, None)
    return jax.shard_map(local, mesh=mesh, in_specs=in_specs, out_specs=out_specs, check_vma=False)
```

```python
import functools

import jax
import jax.numpy as jnp
from jax import lax
from jax.experimental import pallas as pl
from jax.experimental.pallas import tpu as pltpu
from jax.sharding import PartitionSpec as P

MESH = pl.DeviceIdType.MESH
H, KVH, HD = 64, 4, 128
SHARE = H // KVH
NX, NY, NZ = 4, 8, 8
KEYS = 1024
HALF = KEYS // 2
CHUNK = 256
BLOCK = NY // 2 * SHARE
ROWS = 2 * NZ * BLOCK
S_MAX = 256
SUF = S_MAX * 2 * KVH
SCALE = HD**-0.5 * 1.4426950408889634
STAT = 16
PART = ROWS // 2
LOWEST = -1e30
RING = (0, 1, 7, 2, 6, 3, 5, 4)
NEAR = 4
K_NAMES = (
    "right0", "left1", "pair", "relay0", "relay1", "right1", "left0",
    "f10", "f11", "f20", "f21", "f30", "f31",
)
F32, BF16 = jnp.float32, jnp.bfloat16


def place(x, y, z, core):
    return (x * 2 + z % 2, y * 8 + (z // 2) * 2 + core)


def dot_t(a, b):
    return lax.dot_general(a, b, (((1,), (1,)), ((), ())), preferred_element_type=F32)


def to_lanes(column, rows):
    row = lax.broadcasted_iota(jnp.int32, (rows, 128), 0)
    lane = lax.broadcasted_iota(jnp.int32, (rows, 128), 1)
    return jnp.sum(jnp.where(row == lane, column, 0.0), 0, keepdims=True)


def to_rows(line, rows):
    row = lax.broadcasted_iota(jnp.int32, (rows, 128), 0)
    lane = lax.broadcasted_iota(jnp.int32, (rows, 128), 1)
    return jnp.sum(jnp.where(row == lane, line, 0.0), 1, keepdims=True)


def split3(value):
    high = value.astype(BF16).astype(F32)
    middle = (value - high).astype(BF16).astype(F32)
    return high, middle, value - high - middle


def merge(parts):
    best = functools.reduce(jnp.maximum, [p[1] for p in parts])
    weights = [jnp.exp2(p[1] - best) for p in parts]
    total = functools.reduce(jnp.add, weights)
    mixed = functools.reduce(jnp.add, [w * p[0] for w, p in zip(weights, parts)])
    return mixed / total, best + jnp.log2(total)


def suffix_part(q, cached, fresh, length):
    head = lax.broadcasted_iota(jnp.int32, (H, 128), 0) // SHARE
    lane = lax.broadcasted_iota(jnp.int32, (H, 128), 1)
    mine = lane % (2 * KVH) == head
    pieces = SUF // 128
    per_piece = 128 // (2 * KVH)
    low = -jnp.inf
    scores = dot_t(q, cached) * SCALE
    slices = [
        jnp.where(
            mine & (lane // (2 * KVH) + i * per_piece < length),
            scores[:, i * 128 : (i + 1) * 128],
            low,
        )
        for i in range(pieces)
    ]
    slices.append(
        jnp.where(mine & (lane < 2 * KVH), dot_t(q, fresh) * SCALE, low)
    )
    best = jnp.max(functools.reduce(jnp.maximum, slices), -1, keepdims=True)
    weights = [jnp.exp2(s - best).astype(BF16).astype(F32) for s in slices]
    total = jnp.sum(functools.reduce(jnp.add, weights), -1, keepdims=True)
    moved = [pltpu.roll(w, KVH, 1).astype(BF16) for w in weights]
    out = jnp.dot(
        jnp.concatenate(moved[:pieces], 1), cached, preferred_element_type=F32
    ) + jnp.dot(moved[pieces], fresh, preferred_element_type=F32)
    return out / total, best + jnp.log2(total)


def kernel(
    q_ref, kv_ref, suffix_ref, fresh_ref, length_ref, out_ref,
    qall, kvb, cached, fresh, num, den, top, outgoing, returned, ysend, yback,
    y_sem, z_sem, k_sem, zo_sem, yo_sem, local_sem,
):
    def shifted(dx, dy, dz, dcore):
        g, b = lax.axis_index("grp"), lax.axis_index("blk")
        x, z = g // 2, (b % 8) // 2 * 2 + g % 2
        y, core = b // 8, b % 2
        return place((x + dx) % NX, (y + dy) % NY, (z + dz) % NZ, (core + dcore) % 2)

    def along_x(d):
        return shifted(d, 0, 0, 0)

    def along_y(d):
        return shifted(0, d, 0, 0)

    def along_z(d):
        return shifted(0, 0, d, 0)

    y = lax.axis_index("blk") // 8

    def remote(src, dst, sems, i, device):
        return pltpu.make_async_remote_copy(
            src_ref=src, dst_ref=dst, send_sem=sems.at[0, i], recv_sem=sems.at[1, i],
            device_id=device, device_id_type=MESH,
        )

    def kv_copy(name):
        own = {
            "right0": ((0, 0, 0), (1, 0, 0), along_x(1)),
            "left1": ((0, 0, 1), (1, 0, 1), along_x(3)),
            "pair": ((0, 0), (0, 1), shifted(0, 0, 0, 1)),
            "relay0": ((1, 0, 0), (3, 0, 0), along_x(1)),
            "relay1": ((1, 0, 1), (3, 0, 1), along_x(3)),
            "right1": ((0, 0, 1), (2, 0, 0), along_x(1)),
            "left0": ((0, 0, 0), (2, 0, 1), along_x(3)),
        }
        for stage in (1, 2, 3):
            for which in (0, 1):
                own[f"f{stage}{which}"] = (
                    (stage, 0, which), (stage, 1, which), shifted(0, 0, 0, 1)
                )
        src, dst, device = own[name]
        return remote(kvb.at[src], kvb.at[dst], k_sem, K_NAMES.index(name), device)

    def kv_send(*names):
        for name in names:
            kv_copy(name).start()

    def kv_wait(*names):
        for name in names:
            kv_copy(name).wait_recv()

    def z_copy(k, batch):
        return remote(
            qall.at[batch, 0], qall.at[batch, k], z_sem, batch * 8 + k, along_z(RING[k])
        )

    def zo_copy(half, k):
        return remote(
            outgoing.at[half, k], returned.at[half, k], zo_sem, half * 8 + k, along_z(8 - RING[k])
        )

    barrier = pltpu.get_barrier_semaphore()
    partners = [along_x(1), along_x(3), shifted(0, 0, 0, 1)]
    for d in range(1, 8):
        partners += [along_y(d), along_z(d)]
    for device in partners:
        pl.semaphore_signal(barrier, inc=1, device_id=device, device_id_type=MESH)
    own_kv = [
        pltpu.make_async_copy(kv_ref.at[:, pl.ds(h * HALF, HALF)], kvb.at[0, 0, h], local_sem.at[h])
        for h in range(2)
    ]
    for copy in own_kv:
        copy.start()
    own_suffix = pltpu.make_async_copy(suffix_ref, cached, local_sem.at[2])
    own_suffix.start()
    pl.semaphore_wait(barrier, len(partners))

    y_copies = []
    for k in (7, 5, 6, 3, 4, 1, 2):
        d = RING[k]
        rows = pl.ds(pl.multiple_of((y + d) % NY // 2 * SHARE, SHARE), SHARE)
        y_copies.append(
            (k, remote(q_ref.at[rows], qall.at[k // NEAR, 0, pl.ds(k % NEAR * SHARE, SHARE)], y_sem, k, along_y(d)))
        )
        y_copies[-1][1].start()
    mine = pl.ds(pl.multiple_of(y // 2 * SHARE, SHARE), SHARE)
    qall[0, 0, 0:SHARE, :] = q_ref[mine, :]

    for copy in own_kv:
        copy.wait()
    kv_send("right0", "left1", "pair")

    for batch, (lo, hi) in enumerate(((0, NEAR), (NEAR, NY))):
        for k, copy in y_copies:
            if lo <= k < hi:
                copy.wait_recv()
        for k in (7, 5, 6, 3, 4, 1, 2):
            z_copy(k, batch).start()
        if batch == 0:
            kv_send("right1", "left0")

    own_suffix.wait()
    fresh[...] = jnp.zeros_like(fresh)
    fresh[0 : 2 * KVH, :] = fresh_ref[...]
    suffix_out, suffix_log = suffix_part(q_ref[...], cached[...], fresh[...], length_ref[0])

    kv_wait("right0")
    kv_send("relay0")
    kv_wait("left1")
    kv_send("relay1", "f10", "f11")

    def absorb(part, stage):
        rows = pl.ds(pl.multiple_of(part * PART, PART), PART)
        q = qall[part].reshape(PART, HD)
        n, t, best = num[rows, :], den[rows, :], top[rows, :]
        for side in range(2):
            for which in range(2):
                for j in range(HALF // CHUNK):
                    at = slice(j * CHUNK, (j + 1) * CHUNK)
                    keys = kvb[stage, side, which, 0, at, :]
                    values = kvb[stage, side, which, 1, at, :]
                    s = dot_t(q, keys) * SCALE
                    s = [s[:, i : i + 128] for i in range(0, CHUNK, 128)]
                    peak = jnp.max(functools.reduce(jnp.maximum, s), -1, keepdims=True)
                    peak = jnp.maximum(jnp.broadcast_to(peak, (PART, 128)), best)
                    w = [jnp.exp2(i - peak).astype(BF16) for i in s]
                    keep = jnp.exp2(best - peak)
                    n = n * keep + jnp.dot(
                        jnp.concatenate(w, 1), values, preferred_element_type=F32
                    )
                    t = t * keep + functools.reduce(jnp.add, [i.astype(F32) for i in w])
                    best = peak
        num[rows, :], den[rows, :], top[rows, :] = n, t, best

    def normal(half, k):
        rows = slice(half * PART + k * BLOCK, half * PART + (k + 1) * BLOCK)
        total = jnp.broadcast_to(jnp.sum(den[rows, :], -1, keepdims=True), (BLOCK, 128))
        return num[rows, :] / total, top[rows, :] + jnp.log2(total)

    def give_back(half):
        for k in (7, 5, 6, 3, 4, 1, 2):
            average, log = normal(half, k)
            outgoing[half, k, 0:BLOCK, :] = average.astype(BF16)
            lines = jnp.concatenate(
                [*split3(to_lanes(log, BLOCK)), jnp.zeros((STAT - 3, 128), F32)], 0
            )
            outgoing[half, k, BLOCK : BLOCK + STAT, :] = lines.astype(BF16)
            zo_copy(half, k).start()

    num[...] = jnp.zeros_like(num)
    den[...] = jnp.zeros_like(den)
    top[...] = jnp.full(top.shape, LOWEST, F32)
    for k in range(1, NZ):
        z_copy(k, 0).wait_recv()
    kv_wait("pair")

    @pl.loop(0, 5)
    def _(i):
        @pl.when(i == 1)
        def _():
            kv_wait("f10", "f11")

        @pl.when(i == 2)
        def _():
            for k in range(1, NZ):
                z_copy(k, 1).wait_recv()

        @pl.when(i == 3)
        def _():
            kv_wait("right1", "left0")
            kv_send("f20", "f21")

        @pl.when(i == 4)
        def _():
            kv_wait("f20", "f21")

        part = (i + 2) // 4
        absorb(part, i - 2 * part)

    kv_wait("relay0", "relay1")
    kv_send("f30", "f31")

    @pl.loop(0, 3)
    def _(i):
        @pl.when(i == 1)
        def _():
            kv_wait("f30", "f31")

        @pl.when(i == 2)
        def _():
            give_back(1)

        absorb(i % 2, 2 + (i + 1) // 2)

    give_back(0)

    yo_copies = []
    for half in (1, 0):
        parts = [normal(half, 0)]
        for k in (1, 2, 4, 3, 6, 5, 7):
            zo_copy(half, k).wait_recv()
            lines = returned[half, k, BLOCK : BLOCK + STAT, :].astype(F32)
            line = lines[0:1] + lines[1:2] + lines[2:3]
            log = jnp.broadcast_to(to_rows(line, BLOCK), (BLOCK, 128))
            parts.append((returned[half, k, 0:BLOCK, :].astype(F32), log))
        average, log = merge(parts)
        for k in reversed(range(half * NEAR, (half + 1) * NEAR)):
            rows = slice(k % NEAR * SHARE, (k % NEAR + 1) * SHARE)
            line = to_lanes(log[rows], SHARE)
            message = jnp.concatenate([average[rows], jnp.broadcast_to(line, (8, 128))], 0)
            if k == 0:
                yback[y] = message
            else:
                ysend[k] = message
                copy = remote(ysend.at[k], yback.at[y], yo_sem, k, along_y(8 - RING[k]))
                copy.start()
                yo_copies.append(copy)
    for copy in yo_copies:
        copy.wait_recv()
    for head in range(KVH):
        rows = slice(head * SHARE, (head + 1) * SHARE)
        parts = [(suffix_out[rows], suffix_log[rows])]
        for member in (2 * head, 2 * head + 1):
            message = yback[member]
            parts.append((message[:SHARE], to_rows(message[SHARE : SHARE + 1], SHARE)))
        out_ref[rows, :] = merge(parts)[0].astype(BF16)

    for copy in [c for _, c in y_copies] + yo_copies:
        copy.wait_send()
    for k in range(1, NZ):
        z_copy(k, 0).wait_send()
        z_copy(k, 1).wait_send()
        zo_copy(0, k).wait_send()
        zo_copy(1, k).wait_send()
    for name in K_NAMES:
        kv_copy(name).wait_send()


def local(queries, prefix_kv, suffix_kv, new_kv, suffix_len):
    dma = pltpu.SemaphoreType.DMA
    vmem = pl.BlockSpec(memory_space=pltpu.VMEM)
    hbm = pl.BlockSpec(memory_space=pl.ANY)
    out = pl.pallas_call(
        kernel,
        out_shape=jax.ShapeDtypeStruct((H, HD), BF16),
        in_specs=[vmem, hbm, hbm, vmem, pl.BlockSpec(memory_space=pltpu.SMEM)],
        out_specs=vmem,
        scratch_shapes=[
            pltpu.VMEM((2, NZ, BLOCK, HD), BF16),
            pltpu.VMEM((NX, 2, 2, 2, HALF, HD), BF16),
            pltpu.VMEM((SUF, HD), BF16),
            pltpu.VMEM((128, HD), BF16),
            pltpu.VMEM((ROWS, HD), F32),
            pltpu.VMEM((ROWS, 128), F32),
            pltpu.VMEM((ROWS, 128), F32),
            pltpu.VMEM((2, NZ, BLOCK + STAT, HD), BF16),
            pltpu.VMEM((2, NZ, BLOCK + STAT, HD), BF16),
            pltpu.VMEM((NY, SHARE + 8, HD), F32),
            pltpu.VMEM((NY, SHARE + 8, HD), F32),
            dma((2, 8)),
            dma((2, 16)),
            dma((2, 13)),
            dma((2, 16)),
            dma((2, 8)),
            dma((3,)),
        ],
        compiler_params=pltpu.CompilerParams(
            collective_id=0, has_side_effects=True, vmem_limit_bytes=56 * 2**20
        ),
    )(
        queries.reshape(H, HD),
        prefix_kv.reshape(2, KEYS, HD),
        suffix_kv.reshape(SUF, HD),
        new_kv.reshape(2 * KVH, HD),
        suffix_len,
    )
    return out.reshape(1, H, HD)


def solution(mesh):
    in_specs = (
        P(("grp", "blk"), None, None),
        P(None, "grp", "blk", None),
        P(("grp", "blk"), None, None, None, None),
        P(("grp", "blk"), None, None, None),
        P(("grp", "blk")),
    )
    out_specs = P(("grp", "blk"), None, None)
    return jax.shard_map(local, mesh=mesh, in_specs=in_specs, out_specs=out_specs, check_vma=False)
```

```python
import functools

import jax
import jax.numpy as jnp
from jax import lax
from jax.experimental import pallas as pl
from jax.experimental.pallas import tpu as pltpu
from jax.sharding import PartitionSpec as P

MESH = pl.DeviceIdType.MESH
H, KVH, HD = 64, 4, 128
SHARE = H // KVH
NX, NY, NZ = 4, 8, 8
KEYS = 1024
HALF = KEYS // 2
CHUNK = 256
BLOCK = NY // 2 * SHARE
ROWS = 2 * NZ * BLOCK
S_MAX = 256
SUF = S_MAX * 2 * KVH
SCALE = HD**-0.5 * 1.4426950408889634
STAT = 16
PART = ROWS // 2
LOWEST = -1e30
RING = (0, 1, 7, 2, 6, 3, 5, 4)
NEAR = 4
K_NAMES = (
    "right0", "left1", "pair", "relay0", "relay1", "right1", "left0",
    "f10", "f11", "f20", "f21", "f30", "f31",
)
F32, BF16 = jnp.float32, jnp.bfloat16


def place(x, y, z, core):
    return (x * 2 + z % 2, y * 8 + (z // 2) * 2 + core)


def dot_t(a, b):
    return lax.dot_general(a, b, (((1,), (1,)), ((), ())), preferred_element_type=F32)


def to_lanes(column, rows):
    row = lax.broadcasted_iota(jnp.int32, (rows, 128), 0)
    lane = lax.broadcasted_iota(jnp.int32, (rows, 128), 1)
    return jnp.sum(jnp.where(row == lane, column, 0.0), 0, keepdims=True)


def to_rows(line, rows):
    row = lax.broadcasted_iota(jnp.int32, (rows, 128), 0)
    lane = lax.broadcasted_iota(jnp.int32, (rows, 128), 1)
    return jnp.sum(jnp.where(row == lane, line, 0.0), 1, keepdims=True)


def split3(value):
    high = value.astype(BF16).astype(F32)
    middle = (value - high).astype(BF16).astype(F32)
    return high, middle, value - high - middle


def merge(parts):
    best = functools.reduce(jnp.maximum, [p[1] for p in parts])
    weights = [jnp.exp2(p[1] - best) for p in parts]
    total = functools.reduce(jnp.add, weights)
    mixed = functools.reduce(jnp.add, [w * p[0] for w, p in zip(weights, parts)])
    return mixed / total, best + jnp.log2(total)


def suffix_part(q, cached, fresh, length):
    head = lax.broadcasted_iota(jnp.int32, (H, 128), 0) // SHARE
    lane = lax.broadcasted_iota(jnp.int32, (H, 128), 1)
    mine = lane % (2 * KVH) == head
    pieces = SUF // 128
    per_piece = 128 // (2 * KVH)
    low = -jnp.inf
    scores = dot_t(q, cached) * SCALE
    slices = [
        jnp.where(
            mine & (lane // (2 * KVH) + i * per_piece < length),
            scores[:, i * 128 : (i + 1) * 128],
            low,
        )
        for i in range(pieces)
    ]
    slices.append(
        jnp.where(mine & (lane < 2 * KVH), dot_t(q, fresh) * SCALE, low)
    )
    best = jnp.max(functools.reduce(jnp.maximum, slices), -1, keepdims=True)
    weights = [jnp.exp2(s - best).astype(BF16).astype(F32) for s in slices]
    total = jnp.sum(functools.reduce(jnp.add, weights), -1, keepdims=True)
    moved = [pltpu.roll(w, KVH, 1).astype(BF16) for w in weights]
    out = jnp.dot(
        jnp.concatenate(moved[:pieces], 1), cached, preferred_element_type=F32
    ) + jnp.dot(moved[pieces], fresh, preferred_element_type=F32)
    return out / total, best + jnp.log2(total)


def kernel(
    q_ref, kv_ref, suffix_ref, fresh_ref, length_ref, out_ref,
    qall, kvb, cached, fresh, num, den, top, outgoing, returned, ysend, yback,
    y_sem, z_sem, k_sem, zo_sem, yo_sem, local_sem,
):
    def shifted(dx, dy, dz, dcore):
        g, b = lax.axis_index("grp"), lax.axis_index("blk")
        x, z = g // 2, (b % 8) // 2 * 2 + g % 2
        y, core = b // 8, b % 2
        return place((x + dx) % NX, (y + dy) % NY, (z + dz) % NZ, (core + dcore) % 2)

    def along_x(d):
        return shifted(d, 0, 0, 0)

    def along_y(d):
        return shifted(0, d, 0, 0)

    def along_z(d):
        return shifted(0, 0, d, 0)

    y = lax.axis_index("blk") // 8

    def remote(src, dst, sems, i, device):
        return pltpu.make_async_remote_copy(
            src_ref=src, dst_ref=dst, send_sem=sems.at[0, i], recv_sem=sems.at[1, i],
            device_id=device, device_id_type=MESH,
        )

    def kv_copy(name):
        own = {
            "right0": ((0, 0, 0), (1, 0, 0), along_x(1)),
            "left1": ((0, 0, 1), (1, 0, 1), along_x(3)),
            "pair": ((0, 0), (0, 1), shifted(0, 0, 0, 1)),
            "relay0": ((1, 0, 0), (3, 0, 0), along_x(1)),
            "relay1": ((1, 0, 1), (3, 0, 1), along_x(3)),
            "right1": ((0, 0, 1), (2, 0, 0), along_x(1)),
            "left0": ((0, 0, 0), (2, 0, 1), along_x(3)),
        }
        for stage in (1, 2, 3):
            for which in (0, 1):
                own[f"f{stage}{which}"] = (
                    (stage, 0, which), (stage, 1, which), shifted(0, 0, 0, 1)
                )
        src, dst, device = own[name]
        return remote(kvb.at[src], kvb.at[dst], k_sem, K_NAMES.index(name), device)

    def kv_send(*names):
        for name in names:
            kv_copy(name).start()

    def kv_wait(*names):
        for name in names:
            kv_copy(name).wait_recv()

    def z_copy(k, batch):
        return remote(
            qall.at[batch, 0], qall.at[batch, k], z_sem, batch * 8 + k, along_z(RING[k])
        )

    def zo_copy(half, k):
        return remote(
            outgoing.at[half, k], returned.at[half, k], zo_sem, half * 8 + k, along_z(8 - RING[k])
        )

    barrier = pltpu.get_barrier_semaphore()
    partners = [along_x(1), along_x(3), shifted(0, 0, 0, 1)]
    for d in range(1, 8):
        partners += [along_y(d), along_z(d)]
    for device in partners:
        pl.semaphore_signal(barrier, inc=1, device_id=device, device_id_type=MESH)
    own_kv = [
        pltpu.make_async_copy(kv_ref.at[:, pl.ds(h * HALF, HALF)], kvb.at[0, 0, h], local_sem.at[h])
        for h in range(2)
    ]
    for copy in own_kv:
        copy.start()
    own_suffix = pltpu.make_async_copy(suffix_ref, cached, local_sem.at[2])
    own_suffix.start()
    pl.semaphore_wait(barrier, len(partners))

    y_copies = []
    for k in (7, 5, 6, 3, 4, 1, 2):
        d = RING[k]
        rows = pl.ds(pl.multiple_of((y + d) % NY // 2 * SHARE, SHARE), SHARE)
        y_copies.append(
            (k, remote(q_ref.at[rows], qall.at[k // NEAR, 0, pl.ds(k % NEAR * SHARE, SHARE)], y_sem, k, along_y(d)))
        )
        y_copies[-1][1].start()
    mine = pl.ds(pl.multiple_of(y // 2 * SHARE, SHARE), SHARE)
    qall[0, 0, 0:SHARE, :] = q_ref[mine, :]

    for copy in own_kv:
        copy.wait()
    kv_send("right0", "left1", "pair")

    for batch, (lo, hi) in enumerate(((0, NEAR), (NEAR, NY))):
        for k, copy in y_copies:
            if lo <= k < hi:
                copy.wait_recv()
        for k in (7, 5, 6, 3, 4, 1, 2):
            z_copy(k, batch).start()
        if batch == 0:
            kv_send("right1", "left0")

    own_suffix.wait()
    fresh[...] = jnp.zeros_like(fresh)
    fresh[0 : 2 * KVH, :] = fresh_ref[...]
    suffix_out, suffix_log = suffix_part(q_ref[...], cached[...], fresh[...], length_ref[0])

    kv_wait("right0")
    kv_send("relay0")
    kv_wait("left1")
    kv_send("relay1", "f10", "f11")

    def absorb(part, stage):
        rows = pl.ds(pl.multiple_of(part * PART, PART), PART)
        q = qall[part].reshape(PART, HD)
        n, t, best = num[rows, :], den[rows, :], top[rows, :]
        for side in range(2):
            for which in range(2):
                for j in range(HALF // CHUNK):
                    at = slice(j * CHUNK, (j + 1) * CHUNK)
                    keys = kvb[stage, side, which, 0, at, :]
                    values = kvb[stage, side, which, 1, at, :]
                    s = dot_t(q, keys) * SCALE
                    s = [s[:, i : i + 128] for i in range(0, CHUNK, 128)]
                    peak = jnp.max(functools.reduce(jnp.maximum, s), -1, keepdims=True)
                    peak = jnp.maximum(jnp.broadcast_to(peak, (PART, 128)), best)
                    w = [jnp.exp2(i - peak).astype(BF16) for i in s]
                    keep = jnp.exp2(best - peak)
                    n = n * keep + jnp.dot(
                        jnp.concatenate(w, 1), values, preferred_element_type=F32
                    )
                    t = t * keep + functools.reduce(jnp.add, [i.astype(F32) for i in w])
                    best = peak
        num[rows, :], den[rows, :], top[rows, :] = n, t, best

    def normal(half, k):
        rows = slice(half * PART + k * BLOCK, half * PART + (k + 1) * BLOCK)
        total = jnp.broadcast_to(jnp.sum(den[rows, :], -1, keepdims=True), (BLOCK, 128))
        return num[rows, :] / total, top[rows, :] + jnp.log2(total)

    def give_back(half):
        for k in (7, 5, 6, 3, 4, 1, 2):
            average, log = normal(half, k)
            outgoing[half, k, 0:BLOCK, :] = average.astype(BF16)
            lines = jnp.concatenate(
                [*split3(to_lanes(log, BLOCK)), jnp.zeros((STAT - 3, 128), F32)], 0
            )
            outgoing[half, k, BLOCK : BLOCK + STAT, :] = lines.astype(BF16)
            zo_copy(half, k).start()

    num[...] = jnp.zeros_like(num)
    den[...] = jnp.zeros_like(den)
    top[...] = jnp.full(top.shape, LOWEST, F32)
    for k in range(1, NZ):
        z_copy(k, 0).wait_recv()
    kv_wait("pair")

    @pl.loop(0, 8)
    def _(i):
        @pl.when(i == 1)
        def _():
            kv_wait("f10", "f11")

        @pl.when(i == 2)
        def _():
            for k in range(1, NZ):
                z_copy(k, 1).wait_recv()

        @pl.when(i == 3)
        def _():
            kv_wait("right1", "left0")
            kv_send("f20", "f21")

        @pl.when(i == 4)
        def _():
            kv_wait("f20", "f21")

        @pl.when(i == 5)
        def _():
            kv_wait("relay0", "relay1")
            kv_send("f30", "f31")

        @pl.when(i == 6)
        def _():
            kv_wait("f30", "f31")

        @pl.when(i == 7)
        def _():
            give_back(1)

        late = i // 4
        part = (1 - late) * (i // 2) + late * (1 - i % 2)
        absorb(part, (1 - late) * (i % 2) + late * (i // 2))

    give_back(0)

    yo_copies = []
    for half in (1, 0):
        parts = [normal(half, 0)]
        for k in (1, 2, 4, 3, 6, 5, 7):
            zo_copy(half, k).wait_recv()
            lines = returned[half, k, BLOCK : BLOCK + STAT, :].astype(F32)
            line = lines[0:1] + lines[1:2] + lines[2:3]
            log = jnp.broadcast_to(to_rows(line, BLOCK), (BLOCK, 128))
            parts.append((returned[half, k, 0:BLOCK, :].astype(F32), log))
        average, log = merge(parts)
        for k in reversed(range(half * NEAR, (half + 1) * NEAR)):
            rows = slice(k % NEAR * SHARE, (k % NEAR + 1) * SHARE)
            line = to_lanes(log[rows], SHARE)
            message = jnp.concatenate([average[rows], jnp.broadcast_to(line, (8, 128))], 0)
            if k == 0:
                yback[y] = message
            else:
                ysend[k] = message
                copy = remote(ysend.at[k], yback.at[y], yo_sem, k, along_y(8 - RING[k]))
                copy.start()
                yo_copies.append(copy)
    for copy in yo_copies:
        copy.wait_recv()
    for head in range(KVH):
        rows = slice(head * SHARE, (head + 1) * SHARE)
        parts = [(suffix_out[rows], suffix_log[rows])]
        for member in (2 * head, 2 * head + 1):
            message = yback[member]
            parts.append((message[:SHARE], to_rows(message[SHARE : SHARE + 1], SHARE)))
        out_ref[rows, :] = merge(parts)[0].astype(BF16)

    for copy in [c for _, c in y_copies] + yo_copies:
        copy.wait_send()
    for k in range(1, NZ):
        z_copy(k, 0).wait_send()
        z_copy(k, 1).wait_send()
        zo_copy(0, k).wait_send()
        zo_copy(1, k).wait_send()
    for name in K_NAMES:
        kv_copy(name).wait_send()


def local(queries, prefix_kv, suffix_kv, new_kv, suffix_len):
    dma = pltpu.SemaphoreType.DMA
    vmem = pl.BlockSpec(memory_space=pltpu.VMEM)
    hbm = pl.BlockSpec(memory_space=pl.ANY)
    out = pl.pallas_call(
        kernel,
        out_shape=jax.ShapeDtypeStruct((H, HD), BF16),
        in_specs=[vmem, hbm, hbm, vmem, pl.BlockSpec(memory_space=pltpu.SMEM)],
        out_specs=vmem,
        scratch_shapes=[
            pltpu.VMEM((2, NZ, BLOCK, HD), BF16),
            pltpu.VMEM((NX, 2, 2, 2, HALF, HD), BF16),
            pltpu.VMEM((SUF, HD), BF16),
            pltpu.VMEM((128, HD), BF16),
            pltpu.VMEM((ROWS, HD), F32),
            pltpu.VMEM((ROWS, 128), F32),
            pltpu.VMEM((ROWS, 128), F32),
            pltpu.VMEM((2, NZ, BLOCK + STAT, HD), BF16),
            pltpu.VMEM((2, NZ, BLOCK + STAT, HD), BF16),
            pltpu.VMEM((NY, SHARE + 8, HD), F32),
            pltpu.VMEM((NY, SHARE + 8, HD), F32),
            dma((2, 8)),
            dma((2, 16)),
            dma((2, 13)),
            dma((2, 16)),
            dma((2, 8)),
            dma((3,)),
        ],
        compiler_params=pltpu.CompilerParams(
            collective_id=0, has_side_effects=True, vmem_limit_bytes=56 * 2**20
        ),
    )(
        queries.reshape(H, HD),
        prefix_kv.reshape(2, KEYS, HD),
        suffix_kv.reshape(SUF, HD),
        new_kv.reshape(2 * KVH, HD),
        suffix_len,
    )
    return out.reshape(1, H, HD)


def solution(mesh):
    in_specs = (
        P(("grp", "blk"), None, None),
        P(None, "grp", "blk", None),
        P(("grp", "blk"), None, None, None, None),
        P(("grp", "blk"), None, None, None),
        P(("grp", "blk")),
    )
    out_specs = P(("grp", "blk"), None, None)
    return jax.shard_map(local, mesh=mesh, in_specs=in_specs, out_specs=out_specs, check_vma=False)
```
